32 devices in a mesh: grp: 2 (over y), ex: 4 (over z), feat: 4 (over x, core).
Axes of the slice: x: 2, y: 2, z: 4, core: 2. Of those that a mesh axis runs over, the one named last changes fastest.
Arguments:
- queries: bfloat16 [2048, 32768], P(('grp', 'ex'), 'feat'), parts along dimension 0, may hold values from -6 to 6
- grads: bfloat16 [512, 32768], P(('grp', 'ex'), 'feat'), parts along dimension 0, may hold values from -0.03125 to 0.03125
- example_ids: int32 [8, 64], P(('grp', 'ex')), parts along dimension 0, may hold values from 0 to 63, each once within a row
- layer_of_block: int32 [32], P('feat'), may hold values from 0 to 79
- rot_out: bfloat16 [80, 32, 32], replicated, may hold values from -1 to 1
- rot_in: bfloat16 [80, 32, 32], replicated, may hold values from -1 to 1
- eig_out: float32 [80, 32], replicated, may hold values from 0.3 to 3
- eig_in: float32 [80, 32], replicated, may hold values from 0.3 to 3
Outputs:
- scores: float32 [512, 1024], P(('grp', 'ex'), 'feat'), parts along dimension 0
The draws below stay inside these ranges and needn't reach their ends.
There are 2 independent parts, one for each index of `grp`. The reference program is written for one: setup_inputs(seed, part) draws one part's arguments, and reference() takes and returns one part's arrays. A program takes and returns all parts, laid end to end along the dimension named above; an argument that names none is the same for every part. Nothing has to cross between parts.
Inputs may be any that keep to these rules, and one draw needn't show every extreme that they name: Each row of example_ids holds every number of 0 to 63 once.
All inputs are finite; a program needn't handle non-finite values.
Results may differ from the reference program's by a relative error of at most 0.0048.
Values may be sent and summed in bfloat16 or wider, within the bound.
A program may use at most 64 MiB of HBM per device.

```python
import math
import jax
import jax.numpy as jnp
from jax import lax

KOUT = 32
KIN = 32
LAYERS = 80
QB = 256
EX_DEV = 64
STEPS = 3
BLOCKS = 32
FEAT = 32768
QUERIES = 1024
EXAMPLES = 256
N_EX = 4


def touch_ends(values, stream_key, low, largest):
    dims = values.shape
    place = [jax.random.randint(jax.random.fold_in(stream_key, axis), (), 0, dims[axis]) for axis in range(len(dims))]
    values = values.at[tuple(place)].set(low)
    longest = dims.index(max(dims))
    place[longest] = (place[longest] + 1) % dims[longest]
    return values.at[tuple(place)].set(largest)


def shard_levels(key, dims, cuts, low, top_value):
    level = 1.0
    for axis_at, parts in cuts:
        draws = jax.random.uniform(jax.random.fold_in(jax.random.fold_in(key, 6), axis_at), (parts,), jnp.float32, low / len(cuts), top_value / len(cuts))
        level = level * jnp.repeat(jnp.exp(draws), dims[axis_at] // parts).reshape((-1,) + (1,) * (len(dims) - 1 - axis_at))
    return level


def centred(key, extent, deviation, most, cuts=(), kind=jnp.bfloat16):
    array = jax.random.normal(key, extent, jnp.float32) * deviation
    if len(cuts) > 0:
        array = shard_levels(key, extent, cuts, -0.22, 0.18) * array
    return jnp.clip(array, min=-most, max=most).astype(kind)


def setup_inputs(seed: int = 0, part: int = 0) -> dict:
    arg_keys = jax.random.split(jax.random.key(seed), 9)
    own_keys = jax.random.split(jax.random.fold_in(arg_keys[8], part), 9)
    queries = centred(own_keys[0], (QUERIES, FEAT), 1.0, 6.0, ((0, 4), (1, 4)))
    grads = centred(own_keys[1], (EXAMPLES, FEAT), FEAT ** -0.5, 0.03125, ((0, 4), (1, 4)))
    example_ids = jax.vmap(lambda own: jax.random.permutation(own, EX_DEV))(jax.random.split(own_keys[2], N_EX)).reshape((N_EX, EX_DEV)).astype(jnp.int32)
    layer_of_block = touch_ends(jax.random.randint(arg_keys[3], (BLOCKS,), 0, LAYERS), jax.random.fold_in(arg_keys[3], 1), 0, LAYERS - 1).astype(jnp.int32)
    rot_out = centred(arg_keys[4], (LAYERS, KOUT, KOUT), KOUT ** -0.5, 1.0)
    rot_in = centred(arg_keys[5], (LAYERS, KIN, KIN), KIN ** -0.5, 1.0)
    eig_out = jnp.clip(jnp.exp(jax.random.uniform(arg_keys[6], (LAYERS, KOUT), jnp.float32, math.log(0.3), math.log(3.0))), 0.3, 3.0)
    eig_in = jnp.clip(jnp.exp(jax.random.uniform(arg_keys[7], (LAYERS, KIN), jnp.float32, math.log(0.3), math.log(3.0))), 0.3, 3.0)
    return {"queries": queries, "grads": grads, "example_ids": example_ids, "layer_of_block": layer_of_block, "rot_out": rot_out, "rot_in": rot_in, "eig_out": eig_out, "eig_in": eig_in}


DAMPING = 0.1


def precondition(query_rows, out_basis, in_basis, inverse):
    rows = query_rows.shape[0]
    blocks = out_basis.shape[0]
    kout = out_basis.shape[1]
    kin = in_basis.shape[1]
    query_grid = query_rows.reshape(rows, blocks, kout, kin).astype(jnp.float32)
    out_f = out_basis.astype(jnp.float32)
    in_f = in_basis.astype(jnp.float32)
    first_rot = jnp.einsum('bpo,nbpi->boin', out_f, query_grid).astype(jnp.bfloat16)
    second_rot = (jnp.einsum('boin,bij->bojn', first_rot.astype(jnp.float32), in_f) * inverse[:, :, :, None]).astype(jnp.bfloat16)
    third_rot = jnp.einsum('bpo,bojn->bpjn', out_f, second_rot.astype(jnp.float32)).astype(jnp.bfloat16)
    ready = jnp.einsum('bpjn,bij->nbpi', third_rot.astype(jnp.float32), in_f).astype(jnp.bfloat16)
    return ready.reshape(rows, blocks * kout * kin)


def reference(queries, grads, example_ids, layer_of_block, rot_out, rot_in, eig_out, eig_in):
    out_basis = rot_out[layer_of_block]
    in_basis = rot_in[layer_of_block]
    inverse = 1.0 / (eig_out[layer_of_block][:, :, None] * eig_in[layer_of_block][:, None, :] + DAMPING)
    query_shards = queries.reshape(N_EX, QB, FEAT)
    ready_all = lax.map(lambda shard: precondition(shard, out_basis, in_basis, inverse), query_shards)
    grad_shards = grads.reshape(N_EX, EX_DEV, FEAT)

    def one_shard(position):
        local = jnp.take(grad_shards, position, axis=0)
        pieces = []
        for offset in range(STEPS + 1):
            source = jnp.take(ready_all, (position - offset) % N_EX, axis=0)
            pieces.append(jnp.dot(local, source.T, preferred_element_type=jnp.float32))
        raw_rows = jnp.concatenate(pieces, axis=1)
        order = jnp.take(example_ids, position, axis=0)
        return jnp.take(raw_rows, order, axis=0)

    result = lax.map(one_shard, jnp.arange(N_EX, dtype=jnp.int32))
    return result.reshape(N_EX * EX_DEV, (STEPS + 1) * QB)
```

```python
import functools

import jax
import jax.numpy as jnp
from jax import lax
from jax.experimental import pallas as pl
from jax.experimental.pallas import tpu as pltpu
from jax.sharding import PartitionSpec as P

STEPS = 3


DAMPING = 0.1

MESH = pl.DeviceIdType.MESH


def shifted(value, axis, steps):
    count = lax.axis_size(axis)
    pairs = [(source, (source + steps) % count) for source in range(count)]
    return lax.ppermute(value, axis, pairs)


def select_tables(layer_of_block, rot_out, rot_in, eig_out, eig_in):
    levels = jnp.arange(rot_out.shape[0], dtype=jnp.int32)
    onehot = layer_of_block[:, None] == levels[None, :]
    onehot_low = onehot.astype(jnp.bfloat16)
    onehot_full = onehot.astype(jnp.float32)
    out_basis = jnp.einsum(
        "bl,lpo->bpo", onehot_low, rot_out, preferred_element_type=jnp.float32
    ).astype(jnp.bfloat16)
    in_basis = jnp.einsum(
        "bl,lij->bij", onehot_low, rot_in, preferred_element_type=jnp.float32
    ).astype(jnp.bfloat16)
    out_vals = jnp.dot(onehot_full, eig_out, precision=lax.Precision.HIGHEST)
    in_vals = jnp.dot(onehot_full, eig_in, precision=lax.Precision.HIGHEST)
    inverse = 1.0 / (out_vals[:, :, None] * in_vals[:, None, :] + DAMPING)
    return (out_basis, in_basis, inverse)


def precondition(query_rows, out_basis, in_basis, inverse):
    rows = query_rows.shape[0]
    blocks = out_basis.shape[0]
    kout = out_basis.shape[1]
    kin = in_basis.shape[1]
    query_grid = query_rows.reshape(rows, blocks, kout, kin)
    first_rot = jnp.einsum(
        "bpo,nbpi->boin", out_basis, query_grid, preferred_element_type=jnp.float32
    ).astype(jnp.bfloat16)
    second_rot = (
        jnp.einsum("boin,bij->bojn", first_rot, in_basis, preferred_element_type=jnp.float32)
        * inverse[:, :, :, None]
    ).astype(jnp.bfloat16)
    third_rot = jnp.einsum(
        "bpo,bojn->bpjn", out_basis, second_rot, preferred_element_type=jnp.float32
    ).astype(jnp.bfloat16)
    ready = jnp.einsum(
        "bpjn,bij->nbpi", third_rot, in_basis, preferred_element_type=jnp.float32
    ).astype(jnp.bfloat16)
    return ready.reshape(rows, blocks * kout * kin)


def against(query_rows, grads):
    return lax.dot_general(
        query_rows, grads, (((1,), (1,)), ((), ())), preferred_element_type=jnp.float32
    )


def ring_local(queries, grads, example_ids, layer_of_block, rot_out, rot_in, eig_out, eig_in):
    out_basis, in_basis, inverse = select_tables(layer_of_block, rot_out, rot_in, eig_out, eig_in)
    ready = precondition(queries, out_basis, in_basis, inverse)
    current = grads
    pieces = []
    for offset in range(STEPS + 1):
        part = against(ready, current)
        pieces.append(shifted(part, "ex", offset) if offset else part)
        if offset < STEPS:
            current = shifted(current, "ex", -1)
    partial_value = jnp.concatenate(pieces, axis=0)
    owned_rows = lax.psum_scatter(partial_value, "feat", scatter_dimension=0, tiled=True)
    return jnp.take(owned_rows.T, example_ids[0], axis=0)


def dot_nt(a, b):
    return lax.dot_general(a, b, (((1,), (1,)), ((), ())), preferred_element_type=jnp.float32)


def dot_nn(a, b, precision=None):
    return jnp.dot(a, b, preferred_element_type=jnp.float32, precision=precision)


def line_kernel(
    n, kout, kin, cols,
    layer_ref, ids_ref, rot_out_ref, rot_in_ref, eig_out_ref, eig_in_ref, q_hbm, g_hbm,
    out_ref,
    q_buf, ready, x2, basis, u_rows, v_block, g_buf, slots, acc, parts,
    q_sem, g_sem, send_sem, recv_sem, part_send, part_recv,
):
    j = lax.axis_index("ex")
    f = lax.axis_index("feat")
    blocks = ready.shape[0]
    width = kout * kin
    examples = g_buf.shape[1]

    def at(ex, feat):
        return {"ex": ex, "feat": feat}

    def hbm_block(ref, b):
        return ref.at[:, pl.ds(pl.multiple_of(b * width, width), width)]

    def load_q(b):
        return pltpu.make_async_copy(hbm_block(q_hbm, b), q_buf.at[b], q_sem.at[b])

    def load_g(b):
        return pltpu.make_async_copy(hbm_block(g_hbm, b), g_buf.at[b], g_sem.at[b])

    def hop(d, r, b):
        src = hbm_block(g_hbm, b) if r == 0 else slots.at[d, r - 1, b]
        to = jnp.maximum(j - 1, 0) if d == 0 else jnp.minimum(j + 1, n - 1)
        return pltpu.make_async_remote_copy(
            src_ref=src, dst_ref=slots.at[d, r, b],
            send_sem=send_sem.at[d, r, b], recv_sem=recv_sem.at[d, r, b],
            device_id=at(to, f), device_id_type=MESH,
        )

    def sends(d, r):
        if d == 0:
            return jnp.logical_and(j > 0, j + r <= n - 1)
        return jnp.logical_and(j < n - 1, j - r >= 0)

    def receives(d, r):
        if d == 0:
            return j + 1 + r <= n - 1
        return j - 1 - r >= 0

    def send_part(s):
        return pltpu.make_async_remote_copy(
            src_ref=acc.at[s], dst_ref=parts.at[f],
            send_sem=part_send.at[s], recv_sem=part_recv.at[f],
            device_id=at(lax.rem(j + s, n), s), device_id_type=MESH,
        )

    for b in range(blocks):
        load_q(b).start()
        load_g(b).start()

    barrier = pltpu.get_barrier_semaphore()
    for e in range(n):
        for h in range(cols):
            @pl.when(jnp.logical_or(e != j, h != f))
            def _():
                pl.semaphore_signal(barrier, inc=1, device_id=at(e, h), device_id_type=MESH)
    pl.semaphore_wait(barrier, n * cols - 1)

    for b in range(blocks):
        for d in range(2):
            @pl.when(sends(d, 0))
            def _(d=d, b=b):
                hop(d, 0, b).start()

    acc[...] = jnp.zeros_like(acc)

    lane = lax.broadcasted_iota(jnp.int32, (kout, width), 1)
    row = lax.broadcasted_iota(jnp.int32, (kout, width), 0)
    spread_out = (lane // kin == row).astype(jnp.float32)
    spread_in = (lane % kin == row).astype(jnp.float32)
    group = v_block.shape[0]
    reps = group // kin
    lane_group = lax.broadcasted_iota(jnp.int32, (kin, group), 1) // kin
    spread_group = spread_in[:, :group]
    exact = lax.Precision.HIGHEST

    def prepare(b):
        layer = layer_ref[b]
        u = rot_out_ref[layer]
        v = rot_in_ref[layer]
        u_rows[...] = dot_nn(u, spread_out.astype(jnp.bfloat16))
        for p in range(kout):
            basis[p * kin:(p + 1) * kin, :] = (u_rows[p:p + 1, :] * spread_in).astype(jnp.bfloat16)
        v_wide = dot_nn(v, spread_group.astype(jnp.bfloat16))
        for o in range(reps):
            v_block[o * kin:(o + 1) * kin, :] = jnp.where(lane_group == o, v_wide, 0.0).astype(jnp.bfloat16)
        eo = jnp.broadcast_to(eig_out_ref[pl.ds(layer, 1), :], (8, kout))
        ei = jnp.broadcast_to(eig_in_ref[pl.ds(layer, 1), :], (8, kin))
        inverse = 1.0 / (dot_nn(eo, spread_out, exact) * dot_nn(ei, spread_in, exact) + DAMPING)
        inverse = inverse[0:1, :]
        for c in range(width // group):
            here = slice(c * group, (c + 1) * group)
            first = dot_nn(q_buf[b], basis[:, here]).astype(jnp.bfloat16)
            x2[:, here] = (dot_nn(first, v_block[...]) * inverse[:, here]).astype(jnp.bfloat16)
        for c in range(width // group):
            here = slice(c * group, (c + 1) * group)
            third = dot_nt(x2[...], basis[here, :]).astype(jnp.bfloat16)
            ready[b, :, here] = dot_nt(third, v_block[...]).astype(jnp.bfloat16)

    def own(b, _):
        load_q(b).wait()
        load_g(b).wait()
        prepare(b)
        acc[0] += dot_nt(g_buf[b], ready[b])
        return 0

    lax.fori_loop(0, blocks, own, 0)

    @pl.when(f == 0)
    def _():
        parts[0] = acc[0]

    @pl.when(f != 0)
    def _():
        send_part(0).start()

    for r in range(n - 1):
        def step(b, _):
            for d in range(2):
                @pl.when(receives(d, r))
                def _(d=d):
                    hop(d, r, b).wait_recv()
                if r + 1 < n - 1:
                    @pl.when(sends(d, r + 1))
                    def _(d=d):
                        hop(d, r + 1, b).start()
            for d in range(2):
                s = r + 1 if d == 0 else n - 1 - r
                @pl.when(receives(d, r))
                def _(d=d, s=s):
                    acc[s] += dot_nt(slots[d, r, b], ready[b])
            return 0

        lax.fori_loop(0, blocks, step, 0)
        for d in range(2):
            s = r + 1 if d == 0 else n - 1 - r
            @pl.when(receives(d, r))
            def _(s=s):
                send_part(s).start()

    for h in range(cols):
        @pl.when(jnp.logical_not(jnp.logical_and(f == 0, h == 0)))
        def _(h=h):
            pltpu.make_async_remote_copy(
                src_ref=acc.at[0], dst_ref=parts.at[h],
                send_sem=part_send.at[0], recv_sem=part_recv.at[h],
                device_id=at(j, f), device_id_type=MESH,
            ).wait_recv()
    acc_sum = parts[0]
    for h in range(1, cols):
        acc_sum += parts[h]
    parts[0] = acc_sum
    for r in range(examples):
        out_ref[r:r + 1, :] = parts[0, pl.ds(ids_ref[0, r], 1), :]

    @pl.when(f != 0)
    def _():
        send_part(0).wait_send()
    for s in range(1, n):
        send_part(s).wait_send()

    for r in range(n - 1):
        def drain(b, _):
            for d in range(2):
                @pl.when(sends(d, r))
                def _(d=d):
                    hop(d, r, b).wait_send()
            return 0

        lax.fori_loop(0, blocks, drain, 0)


def line_local(n, cols, queries, grads, example_ids, layer_of_block, rot_out, rot_in, eig_out, eig_in):
    rows = queries.shape[0]
    examples = grads.shape[0]
    blocks = layer_of_block.shape[0]
    kout, kin = rot_out.shape[1], rot_in.shape[1]
    width = kout * kin
    group = min(256, width)
    bf16, f32 = jnp.bfloat16, jnp.float32
    smem = pl.BlockSpec(memory_space=pltpu.SMEM)
    vmem = pl.BlockSpec(memory_space=pltpu.VMEM)
    hbm = pl.BlockSpec(memory_space=pl.ANY)
    return pl.pallas_call(
        functools.partial(line_kernel, n, kout, kin, cols),
        out_shape=jax.ShapeDtypeStruct((examples, rows), f32),
        in_specs=[smem, smem, vmem, vmem, vmem, vmem, hbm, hbm],
        out_specs=vmem,
        scratch_shapes=[
            pltpu.VMEM((blocks, rows, width), bf16),
            pltpu.VMEM((blocks, rows, width), bf16),
            pltpu.VMEM((rows, width), bf16),
            pltpu.VMEM((width, width), bf16),
            pltpu.VMEM((kout, width), f32),
            pltpu.VMEM((group, group), bf16),
            pltpu.VMEM((blocks, examples, width), bf16),
            pltpu.VMEM((2, n - 1, blocks, examples, width), bf16),
            pltpu.VMEM((n, examples, rows), f32),
            pltpu.VMEM((cols, examples, rows), f32),
            pltpu.SemaphoreType.DMA((blocks,)),
            pltpu.SemaphoreType.DMA((blocks,)),
            pltpu.SemaphoreType.DMA((2, n - 1, blocks)),
            pltpu.SemaphoreType.DMA((2, n - 1, blocks)),
            pltpu.SemaphoreType.DMA((n,)),
            pltpu.SemaphoreType.DMA((cols,)),
        ],
        compiler_params=pltpu.CompilerParams(
            collective_id=0, has_side_effects=True, vmem_limit_bytes=40 * 1024 * 1024
        ),
    )(layer_of_block, example_ids, rot_out, rot_in, eig_out, eig_in, queries, grads)


def solution(mesh):
    in_specs = (
        P(("grp", "ex"), "feat"),
        P(("grp", "ex"), "feat"),
        P(("grp", "ex"), None),
        P("feat"),
        P(),
        P(),
        P(),
        P(),
    )
    out_specs = P(("grp", "ex"), "feat")
    n, cols = mesh.shape["ex"], mesh.shape["feat"]
    local = functools.partial(line_local, n, cols) if n == cols == STEPS + 1 else ring_local
    return jax.shard_map(local, mesh=mesh, in_specs=in_specs, out_specs=out_specs, check_vma=False)
```

```python
import functools

import jax
import jax.numpy as jnp
from jax import lax
from jax.experimental import pallas as pl
from jax.experimental.pallas import tpu as pltpu
from jax.sharding import PartitionSpec as P

STEPS = 3


DAMPING = 0.1

MESH = pl.DeviceIdType.MESH


def shifted(value, axis, steps):
    count = lax.axis_size(axis)
    pairs = [(source, (source + steps) % count) for source in range(count)]
    return lax.ppermute(value, axis, pairs)


def select_tables(layer_of_block, rot_out, rot_in, eig_out, eig_in):
    levels = jnp.arange(rot_out.shape[0], dtype=jnp.int32)
    onehot = layer_of_block[:, None] == levels[None, :]
    onehot_low = onehot.astype(jnp.bfloat16)
    onehot_full = onehot.astype(jnp.float32)
    out_basis = jnp.einsum(
        "bl,lpo->bpo", onehot_low, rot_out, preferred_element_type=jnp.float32
    ).astype(jnp.bfloat16)
    in_basis = jnp.einsum(
        "bl,lij->bij", onehot_low, rot_in, preferred_element_type=jnp.float32
    ).astype(jnp.bfloat16)
    out_vals = jnp.dot(onehot_full, eig_out, precision=lax.Precision.HIGHEST)
    in_vals = jnp.dot(onehot_full, eig_in, precision=lax.Precision.HIGHEST)
    inverse = 1.0 / (out_vals[:, :, None] * in_vals[:, None, :] + DAMPING)
    return (out_basis, in_basis, inverse)


def precondition(query_rows, out_basis, in_basis, inverse):
    rows = query_rows.shape[0]
    blocks = out_basis.shape[0]
    kout = out_basis.shape[1]
    kin = in_basis.shape[1]
    query_grid = query_rows.reshape(rows, blocks, kout, kin)
    first_rot = jnp.einsum(
        "bpo,nbpi->boin", out_basis, query_grid, preferred_element_type=jnp.float32
    ).astype(jnp.bfloat16)
    second_rot = (
        jnp.einsum("boin,bij->bojn", first_rot, in_basis, preferred_element_type=jnp.float32)
        * inverse[:, :, :, None]
    ).astype(jnp.bfloat16)
    third_rot = jnp.einsum(
        "bpo,bojn->bpjn", out_basis, second_rot, preferred_element_type=jnp.float32
    ).astype(jnp.bfloat16)
    ready = jnp.einsum(
        "bpjn,bij->nbpi", third_rot, in_basis, preferred_element_type=jnp.float32
    ).astype(jnp.bfloat16)
    return ready.reshape(rows, blocks * kout * kin)


def against(query_rows, grads):
    return lax.dot_general(
        query_rows, grads, (((1,), (1,)), ((), ())), preferred_element_type=jnp.float32
    )


def ring_local(queries, grads, example_ids, layer_of_block, rot_out, rot_in, eig_out, eig_in):
    out_basis, in_basis, inverse = select_tables(layer_of_block, rot_out, rot_in, eig_out, eig_in)
    ready = precondition(queries, out_basis, in_basis, inverse)
    current = grads
    pieces = []
    for offset in range(STEPS + 1):
        part = against(ready, current)
        pieces.append(shifted(part, "ex", offset) if offset else part)
        if offset < STEPS:
            current = shifted(current, "ex", -1)
    partial_value = jnp.concatenate(pieces, axis=0)
    owned_rows = lax.psum_scatter(partial_value, "feat", scatter_dimension=0, tiled=True)
    return jnp.take(owned_rows.T, example_ids[0], axis=0)


def dot_nt(a, b):
    return lax.dot_general(a, b, (((1,), (1,)), ((), ())), preferred_element_type=jnp.float32)


def dot_nn(a, b, precision=None):
    return jnp.dot(a, b, preferred_element_type=jnp.float32, precision=precision)


def line_kernel(
    n, kout, kin, cols, keep,
    layer_ref, ids_ref, rot_out_hbm, rot_in_hbm, eig_out_hbm, eig_in_hbm, q_hbm, g_hbm,
    out_ref,
    rot_out_t, rot_in_t, eig_out_t, eig_in_t, u_tab, v_tab, inv_tab,
    q_buf, ready, x2, basis, u_rows, v_block, g_buf, slots, acc, parts,
    far_q, far_ready, far_acc, far_parts,
    table_sem, q_sem, g_sem, send_sem, recv_sem, part_send, part_recv,
    far_send, far_recv, far_part_send, far_part_recv,
):
    j = lax.axis_index("ex")
    f = lax.axis_index("feat")
    blocks = ready.shape[0]
    width = kout * kin
    examples = g_buf.shape[1]
    layers = rot_out_t.shape[1]
    exact = lax.Precision.HIGHEST

    def at(ex, feat):
        return {"ex": ex, "feat": feat}

    def hbm_block(ref, b):
        if not isinstance(b, int):
            b = pl.multiple_of(b * width, width)
        else:
            b = b * width
        return ref.at[:, pl.ds(b, width)]

    def load_q(b):
        return pltpu.make_async_copy(hbm_block(q_hbm, b), q_buf.at[b], q_sem.at[b])

    def load_g(b):
        return pltpu.make_async_copy(hbm_block(g_hbm, b), g_buf.at[b], g_sem.at[b])

    def hop(d, r, b):
        src = hbm_block(g_hbm, b) if r == 0 else slots.at[d, r - 1, b]
        to = jnp.maximum(j - 1, 0) if d == 0 else jnp.minimum(j + 1, n - 1)
        return pltpu.make_async_remote_copy(
            src_ref=src, dst_ref=slots.at[d, r, b],
            send_sem=send_sem.at[d, r, b], recv_sem=recv_sem.at[d, r, b],
            device_id=at(to, f), device_id_type=MESH,
        )

    def sends(d, r, b):
        if d == 0:
            there = jnp.logical_and(j > 0, j + r <= n - 1)
            return jnp.logical_and(there, jnp.logical_or(j != 1, b < keep))
        there = jnp.logical_and(j < n - 1, j - r >= 0)
        return jnp.logical_and(there, jnp.logical_or(j != n - 2, b < keep))

    def receives(d, r, b):
        if d == 0:
            return jnp.logical_and(j + 1 + r <= n - 1, jnp.logical_or(j != 0, b < keep))
        return jnp.logical_and(j - 1 - r >= 0, jnp.logical_or(j != n - 1, b < keep))

    def far(m):
        return pltpu.make_async_remote_copy(
            src_ref=hbm_block(q_hbm, keep + m), dst_ref=far_q.at[m],
            send_sem=far_send.at[m], recv_sem=far_recv.at[m],
            device_id=at(jnp.where(j < 2, 1, n - 2), f), device_id_type=MESH,
        )

    is_end = jnp.logical_or(j == 0, j == n - 1)
    is_helper = jnp.logical_or(j == 1, j == n - 2)
    low = j == 1

    def send_part(s):
        return pltpu.make_async_remote_copy(
            src_ref=acc.at[s], dst_ref=parts.at[f],
            send_sem=part_send.at[s], recv_sem=part_recv.at[f],
            device_id=at(lax.rem(j + s, n), s), device_id_type=MESH,
        )

    def far_feat(t):
        return jnp.where(low, 1 + t, n - 1 - t)

    def send_far_part(t):
        return pltpu.make_async_remote_copy(
            src_ref=far_acc.at[t], dst_ref=far_parts.at[f],
            send_sem=far_part_send.at[t], recv_sem=far_part_recv.at[f],
            device_id=at(jnp.where(low, 1 + t, n - 2 - t), far_feat(t)), device_id_type=MESH,
        )

    tables = [
        pltpu.make_async_copy(src, dst, table_sem.at[i])
        for i, (src, dst) in enumerate([
            (rot_out_hbm, rot_out_t), (rot_in_hbm, rot_in_t),
            (eig_out_hbm, eig_out_t), (eig_in_hbm, eig_in_t),
        ])
    ]

    barrier = pltpu.get_barrier_semaphore()
    for e in range(n):
        for h in range(cols):
            @pl.when(jnp.logical_or(e != j, h != f))
            def _():
                pl.semaphore_signal(barrier, inc=1, device_id=at(e, h), device_id_type=MESH)
    for table in tables:
        table.start()
    for b in range(blocks):
        load_q(b).start()
        load_g(b).start()
    pl.semaphore_wait(barrier, n * cols - 1)

    moved = blocks - keep
    for b in range(blocks):
        for d in range(2):
            @pl.when(sends(d, 0, b))
            def _(d=d, b=b):
                hop(d, 0, b).start()
        if (b + 1) * moved % blocks == 0:
            @pl.when(is_end)
            def _(m=(b + 1) * moved // blocks - 1):
                far(m).start()

    acc[...] = jnp.zeros_like(acc)
    far_acc[...] = jnp.zeros_like(far_acc)

    lane = lax.broadcasted_iota(jnp.int32, (kout, width), 1)
    row = lax.broadcasted_iota(jnp.int32, (kout, width), 0)
    spread_out = (lane // kin == row).astype(jnp.float32)
    spread_in = (lane % kin == row).astype(jnp.float32)
    group = v_block.shape[0]
    reps = group // kin
    lane_group = lax.broadcasted_iota(jnp.int32, (kin, group), 1) // kin
    spread_group = spread_in[:, :group]

    level = lax.broadcasted_iota(jnp.int32, (blocks, layers), 1)
    which = lax.broadcasted_iota(jnp.int32, (blocks, layers), 0)
    onehot = jnp.zeros((blocks, layers), jnp.float32)
    for b in range(blocks):
        onehot = jnp.where(jnp.logical_and(which == b, level == layer_ref[b]), 1.0, onehot)
    for table in tables:
        table.wait()
    for ref, tab, rows in ((rot_out_t, u_tab, kout), (rot_in_t, v_tab, kin)):
        flat = dot_nt(onehot.astype(jnp.bfloat16), ref[...])
        for p in range(rows):
            piece = flat[:, p * rows:(p + 1) * rows]
            for b in range(blocks):
                tab[b, p:p + 1, :] = piece[b:b + 1, :]
    dot_nt_exact = functools.partial(
        lax.dot_general, dimension_numbers=(((1,), (1,)), ((), ())),
        precision=exact, preferred_element_type=jnp.float32,
    )
    eo = dot_nt_exact(onehot, eig_out_t[...])
    ei = dot_nt_exact(onehot, eig_in_t[...])
    inv_tab[...] = 1.0 / (dot_nn(eo, spread_out, exact) * dot_nn(ei, spread_in, exact) + DAMPING)

    def prepare(b, src, dst, slot):
        u_rows[...] = dot_nn(u_tab[b].astype(jnp.bfloat16), spread_out.astype(jnp.bfloat16))
        for p in range(kout):
            basis[p * kin:(p + 1) * kin, :] = (u_rows[p:p + 1, :] * spread_in).astype(jnp.bfloat16)
        v_wide = dot_nn(v_tab[b].astype(jnp.bfloat16), spread_group.astype(jnp.bfloat16))
        for o in range(reps):
            v_block[o * kin:(o + 1) * kin, :] = jnp.where(lane_group == o, v_wide, 0.0).astype(jnp.bfloat16)
        inverse = inv_tab[pl.ds(b, 1), :]
        for c in range(width // group):
            here = slice(c * group, (c + 1) * group)
            first = dot_nn(src[slot], basis[:, here]).astype(jnp.bfloat16)
            x2[:, here] = (dot_nn(first, v_block[...]) * inverse[:, here]).astype(jnp.bfloat16)
        for c in range(width // group):
            here = slice(c * group, (c + 1) * group)
            third = dot_nt(x2[...], basis[here, :]).astype(jnp.bfloat16)
            dst[slot, :, here] = dot_nt(third, v_block[...]).astype(jnp.bfloat16)

    def step(r, b):
        for d in range(2):
            @pl.when(receives(d, r, b))
            def _(d=d):
                hop(d, r, b).wait_recv()
            if r + 1 < n - 1:
                @pl.when(sends(d, r + 1, b))
                def _(d=d):
                    hop(d, r + 1, b).start()
        for d in range(2):
            s = r + 1 if d == 0 else n - 1 - r
            @pl.when(receives(d, r, b))
            def _(d=d, s=s):
                acc[s] += dot_nt(slots[d, r, b], ready[b])

    def finish(r):
        for d in range(2):
            s = r + 1 if d == 0 else n - 1 - r
            @pl.when(receives(d, r, 0))
            def _(s=s):
                send_part(s).start()

    def own(b, _):
        load_q(b).wait()
        load_g(b).wait()
        prepare(b, q_buf, ready, b)
        acc[0] += dot_nt(g_buf[b], ready[b])
        step(0, b)
        return 0

    def later(r):
        def body(b, _):
            step(r, b)
            return 0

        lax.fori_loop(0, blocks, body, 0)
        finish(r)

    lax.fori_loop(0, blocks, own, 0)

    @pl.when(f == 0)
    def _():
        parts[0] = acc[0]

    @pl.when(f != 0)
    def _():
        send_part(0).start()

    finish(0)

    def help_out(m):
        @pl.when(is_helper)
        def _():
            far(m).wait_recv()
            prepare(keep + m, far_q, far_ready, m)

    half = moved // 2
    for m in range(half):
        help_out(m)
    later(1)
    for m in range(half, moved):
        help_out(m)

    @pl.when(is_helper)
    def _():
        side = jnp.where(low, 0, 1)
        for m in range(moved):
            far_acc[0] += dot_nt(g_buf[keep + m], far_ready[m])
            for r in range(n - 2):
                far_acc[1 + r] += dot_nt(slots[side, r, keep + m], far_ready[m])

    for t in range(n - 1):
        here = jnp.logical_and(t == 0, far_feat(t) == f)

        @pl.when(jnp.logical_and(is_helper, here))
        def _(t=t):
            far_parts[pl.ds(f, 1)] = far_acc[t:t + 1]

        @pl.when(jnp.logical_and(is_helper, jnp.logical_not(here)))
        def _(t=t):
            send_far_part(t).start()

    later(2)

    def arrived(ref, sem, h):
        return pltpu.make_async_remote_copy(
            src_ref=acc.at[0], dst_ref=ref.at[h],
            send_sem=part_send.at[0], recv_sem=sem.at[h],
            device_id=at(j, f), device_id_type=MESH,
        )

    k = lax.rem(j - f + n, n)
    split = jnp.logical_and(f != 0, jnp.logical_or(k == 0, k == n - 1))
    helper_of = jnp.where(k == 0, 1, n - 2)

    @pl.when(split)
    def _():
        for h in range(cols):
            @pl.when(jnp.logical_or(helper_of != j, h != f))
            def _(h=h):
                arrived(far_parts, far_part_recv, h).wait_recv()
        total = far_parts[0]
        for h in range(1, cols):
            total += far_parts[h]
        far_acc[n - 1] = total

    for h in range(cols):
        @pl.when(jnp.logical_not(jnp.logical_and(f == 0, h == 0)))
        def _(h=h):
            arrived(parts, part_recv, h).wait_recv()
    total = far_acc[n - 1] + parts[0]
    for h in range(1, cols):
        total += parts[h]
    parts[0] = total
    for r in range(examples):
        out_ref[r:r + 1, :] = parts[0, pl.ds(ids_ref[0, r], 1), :]

    @pl.when(f != 0)
    def _():
        send_part(0).wait_send()
    for s in range(1, n):
        send_part(s).wait_send()
    for t in range(n - 1):
        here = jnp.logical_and(t == 0, far_feat(t) == f)

        @pl.when(jnp.logical_and(is_helper, jnp.logical_not(here)))
        def _(t=t):
            send_far_part(t).wait_send()

    @pl.when(is_end)
    def _():
        for m in range(moved):
            far(m).wait_send()

    for r in range(n - 1):
        def drain(b, _):
            for d in range(2):
                @pl.when(sends(d, r, b))
                def _(d=d):
                    hop(d, r, b).wait_send()
            return 0

        lax.fori_loop(0, blocks, drain, 0)


def line_local(n, cols, queries, grads, example_ids, layer_of_block, rot_out, rot_in, eig_out, eig_in):
    rows = queries.shape[0]
    examples = grads.shape[0]
    blocks = layer_of_block.shape[0]
    layers, kout, kin = rot_out.shape[0], rot_out.shape[1], rot_in.shape[1]
    width = kout * kin
    group = min(256, width)
    keep = blocks - blocks // 4
    moved = blocks - keep
    bf16, f32 = jnp.bfloat16, jnp.float32
    smem = pl.BlockSpec(memory_space=pltpu.SMEM)
    vmem = pl.BlockSpec(memory_space=pltpu.VMEM)
    hbm = pl.BlockSpec(memory_space=pl.ANY)
    dma = pltpu.SemaphoreType.DMA
    return pl.pallas_call(
        functools.partial(line_kernel, n, kout, kin, cols, keep),
        out_shape=jax.ShapeDtypeStruct((examples, rows), f32),
        in_specs=[smem, smem] + [hbm] * 6,
        out_specs=vmem,
        scratch_shapes=[
            pltpu.VMEM((kout * kout, layers), bf16),
            pltpu.VMEM((kin * kin, layers), bf16),
            pltpu.VMEM((kout, layers), f32),
            pltpu.VMEM((kin, layers), f32),
            pltpu.VMEM((blocks, kout, kout), f32),
            pltpu.VMEM((blocks, kin, kin), f32),
            pltpu.VMEM((blocks, width), f32),
            pltpu.VMEM((blocks, rows, width), bf16),
            pltpu.VMEM((blocks, rows, width), bf16),
            pltpu.VMEM((rows, width), bf16),
            pltpu.VMEM((width, width), bf16),
            pltpu.VMEM((kout, width), f32),
            pltpu.VMEM((group, group), bf16),
            pltpu.VMEM((blocks, examples, width), bf16),
            pltpu.VMEM((2, n - 1, blocks, examples, width), bf16),
            pltpu.VMEM((n, examples, rows), f32),
            pltpu.VMEM((cols, examples, rows), f32),
            pltpu.VMEM((moved, rows, width), bf16),
            pltpu.VMEM((moved, rows, width), bf16),
            pltpu.VMEM((n, examples, rows), f32),
            pltpu.VMEM((cols, examples, rows), f32),
            dma((4,)),
            dma((blocks,)),
            dma((blocks,)),
            dma((2, n - 1, blocks)),
            dma((2, n - 1, blocks)),
            dma((n,)),
            dma((cols,)),
            dma((moved,)),
            dma((moved,)),
            dma((n - 1,)),
            dma((cols,)),
        ],
        compiler_params=pltpu.CompilerParams(
            collective_id=0, has_side_effects=True, vmem_limit_bytes=58 * 1024 * 1024
        ),
    )(
        layer_of_block, example_ids,
        rot_out.transpose(1, 2, 0).reshape(kout * kout, layers),
        rot_in.transpose(1, 2, 0).reshape(kin * kin, layers),
        eig_out.T, eig_in.T, queries, grads,
    )


def solution(mesh):
    in_specs = (
        P(("grp", "ex"), "feat"),
        P(("grp", "ex"), "feat"),
        P(("grp", "ex"), None),
        P("feat"),
        P(),
        P(),
        P(),
        P(),
    )
    out_specs = P(("grp", "ex"), "feat")
    n, cols = mesh.shape["ex"], mesh.shape["feat"]
    local = functools.partial(line_local, n, cols) if n == cols == STEPS + 1 else ring_local
    return jax.shard_map(local, mesh=mesh, in_specs=in_specs, out_specs=out_specs, check_vma=False)
```

```python
import functools

import jax
import jax.numpy as jnp
from jax import lax
from jax.experimental import pallas as pl
from jax.experimental.pallas import tpu as pltpu
from jax.sharding import PartitionSpec as P

STEPS = 3


DAMPING = 0.1

MESH = pl.DeviceIdType.MESH


def shifted(value, axis, steps):
    count = lax.axis_size(axis)
    pairs = [(source, (source + steps) % count) for source in range(count)]
    return lax.ppermute(value, axis, pairs)


def select_tables(layer_of_block, rot_out, rot_in, eig_out, eig_in):
    levels = jnp.arange(rot_out.shape[0], dtype=jnp.int32)
    onehot = layer_of_block[:, None] == levels[None, :]
    onehot_low = onehot.astype(jnp.bfloat16)
    onehot_full = onehot.astype(jnp.float32)
    out_basis = jnp.einsum(
        "bl,lpo->bpo", onehot_low, rot_out, preferred_element_type=jnp.float32
    ).astype(jnp.bfloat16)
    in_basis = jnp.einsum(
        "bl,lij->bij", onehot_low, rot_in, preferred_element_type=jnp.float32
    ).astype(jnp.bfloat16)
    out_vals = jnp.dot(onehot_full, eig_out, precision=lax.Precision.HIGHEST)
    in_vals = jnp.dot(onehot_full, eig_in, precision=lax.Precision.HIGHEST)
    inverse = 1.0 / (out_vals[:, :, None] * in_vals[:, None, :] + DAMPING)
    return (out_basis, in_basis, inverse)


def precondition(query_rows, out_basis, in_basis, inverse):
    rows = query_rows.shape[0]
    blocks = out_basis.shape[0]
    kout = out_basis.shape[1]
    kin = in_basis.shape[1]
    query_grid = query_rows.reshape(rows, blocks, kout, kin)
    first_rot = jnp.einsum(
        "bpo,nbpi->boin", out_basis, query_grid, preferred_element_type=jnp.float32
    ).astype(jnp.bfloat16)
    second_rot = (
        jnp.einsum("boin,bij->bojn", first_rot, in_basis, preferred_element_type=jnp.float32)
        * inverse[:, :, :, None]
    ).astype(jnp.bfloat16)
    third_rot = jnp.einsum(
        "bpo,bojn->bpjn", out_basis, second_rot, preferred_element_type=jnp.float32
    ).astype(jnp.bfloat16)
    ready = jnp.einsum(
        "bpjn,bij->nbpi", third_rot, in_basis, preferred_element_type=jnp.float32
    ).astype(jnp.bfloat16)
    return ready.reshape(rows, blocks * kout * kin)


def against(query_rows, grads):
    return lax.dot_general(
        query_rows, grads, (((1,), (1,)), ((), ())), preferred_element_type=jnp.float32
    )


def ring_local(queries, grads, example_ids, layer_of_block, rot_out, rot_in, eig_out, eig_in):
    out_basis, in_basis, inverse = select_tables(layer_of_block, rot_out, rot_in, eig_out, eig_in)
    ready = precondition(queries, out_basis, in_basis, inverse)
    current = grads
    pieces = []
    for offset in range(STEPS + 1):
        part = against(ready, current)
        pieces.append(shifted(part, "ex", offset) if offset else part)
        if offset < STEPS:
            current = shifted(current, "ex", -1)
    partial_value = jnp.concatenate(pieces, axis=0)
    owned_rows = lax.psum_scatter(partial_value, "feat", scatter_dimension=0, tiled=True)
    return jnp.take(owned_rows.T, example_ids[0], axis=0)


def dot_nt(a, b):
    return lax.dot_general(a, b, (((1,), (1,)), ((), ())), preferred_element_type=jnp.float32)


def dot_nn(a, b, precision=None):
    return jnp.dot(a, b, preferred_element_type=jnp.float32, precision=precision)


def line_kernel(
    n, kout, kin, cols, moved,
    layer_ref, ids_ref, rot_out_hbm, rot_in_hbm, eig_out_hbm, eig_in_hbm, q_hbm, g_hbm,
    out_ref,
    rot_out_t, rot_in_t, eig_out_t, eig_in_t, u_tab, v_tab, inv_tab,
    q_buf, ready, x2, basis, u_rows, v_block, g_buf, slots, acc, parts,
    far_ready, far_acc, far_parts, packed, far_packed,
    table_sem, q_sem, g_sem, send_sem, recv_sem, part_send, part_recv,
    far_send, far_recv, far_part_send, far_part_recv,
):
    j = lax.axis_index("ex")
    f = lax.axis_index("feat")
    blocks = ready.shape[0]
    width = kout * kin
    examples = g_buf.shape[1]
    layers = rot_out_t.shape[1]
    exact = lax.Precision.HIGHEST

    def at(ex, feat):
        return {"ex": ex, "feat": feat}

    def hbm_block(ref, b):
        if not isinstance(b, int):
            b = pl.multiple_of(b * width, width)
        else:
            b = b * width
        return ref.at[:, pl.ds(b, width)]

    def load_q(b):
        return pltpu.make_async_copy(hbm_block(q_hbm, b), q_buf.at[b], q_sem.at[b])

    def load_g(b):
        return pltpu.make_async_copy(hbm_block(g_hbm, b), g_buf.at[b], g_sem.at[b])

    def hop(d, r, b):
        src = hbm_block(g_hbm, b) if r == 0 else slots.at[d, r - 1, b]
        to = jnp.maximum(j - 1, 0) if d == 0 else jnp.minimum(j + 1, n - 1)
        return pltpu.make_async_remote_copy(
            src_ref=src, dst_ref=slots.at[d, r, b],
            send_sem=send_sem.at[d, r, b], recv_sem=recv_sem.at[d, r, b],
            device_id=at(to, f), device_id_type=MESH,
        )

    def sends(d, r, b):
        if d == 0:
            there = jnp.logical_and(j > 0, j + r <= n - 1)
            return jnp.logical_and(there, jnp.logical_or(j != 1, b >= moved))
        there = jnp.logical_and(j < n - 1, j - r >= 0)
        return jnp.logical_and(there, jnp.logical_or(j != n - 2, b >= moved))

    def receives(d, r, b):
        if d == 0:
            return jnp.logical_and(j + 1 + r <= n - 1, jnp.logical_or(j != 0, b >= moved))
        return jnp.logical_and(j - 1 - r >= 0, jnp.logical_or(j != n - 1, b >= moved))

    def far(m):
        return pltpu.make_async_remote_copy(
            src_ref=ready.at[m], dst_ref=far_ready.at[m],
            send_sem=far_send.at[m], recv_sem=far_recv.at[m],
            device_id=at(jnp.where(j < 2, 1, n - 2), f), device_id_type=MESH,
        )

    is_end = jnp.logical_or(j == 0, j == n - 1)
    is_helper = jnp.logical_or(j == 1, j == n - 2)
    low = j == 1

    def send_part(s):
        return pltpu.make_async_remote_copy(
            src_ref=packed.at[s], dst_ref=parts.at[f],
            send_sem=part_send.at[s], recv_sem=part_recv.at[f],
            device_id=at(lax.rem(j + s, n), s), device_id_type=MESH,
        )

    def far_feat(t):
        return jnp.where(low, 1 + t, n - 1 - t)

    def send_far_part(t):
        return pltpu.make_async_remote_copy(
            src_ref=far_packed.at[t], dst_ref=far_parts.at[f],
            send_sem=far_part_send.at[t], recv_sem=far_part_recv.at[f],
            device_id=at(jnp.where(low, 1 + t, n - 2 - t), far_feat(t)), device_id_type=MESH,
        )

    tables = [
        pltpu.make_async_copy(src, dst, table_sem.at[i])
        for i, (src, dst) in enumerate([
            (rot_out_hbm, rot_out_t), (rot_in_hbm, rot_in_t),
            (eig_out_hbm, eig_out_t), (eig_in_hbm, eig_in_t),
        ])
    ]

    barrier = pltpu.get_barrier_semaphore()
    for e in range(n):
        for h in range(cols):
            @pl.when(jnp.logical_or(e != j, h != f))
            def _():
                pl.semaphore_signal(barrier, inc=1, device_id=at(e, h), device_id_type=MESH)
    for table in tables:
        table.start()
    for b in range(blocks):
        load_q(b).start()
        load_g(b).start()
    pl.semaphore_wait(barrier, n * cols - 1)

    for b in range(blocks):
        for d in range(2):
            @pl.when(sends(d, 0, b))
            def _(d=d, b=b):
                hop(d, 0, b).start()

    acc[...] = jnp.zeros_like(acc)
    far_acc[...] = jnp.zeros_like(far_acc)

    lane = lax.broadcasted_iota(jnp.int32, (kout, width), 1)
    row = lax.broadcasted_iota(jnp.int32, (kout, width), 0)
    spread_out = (lane // kin == row).astype(jnp.float32)
    spread_in = (lane % kin == row).astype(jnp.float32)
    group = v_block.shape[0]
    reps = group // kin
    lane_group = lax.broadcasted_iota(jnp.int32, (kin, group), 1) // kin
    spread_group = spread_in[:, :group]

    level = lax.broadcasted_iota(jnp.int32, (blocks, layers), 1)
    which = lax.broadcasted_iota(jnp.int32, (blocks, layers), 0)
    onehot = jnp.zeros((blocks, layers), jnp.float32)
    for b in range(blocks):
        onehot = jnp.where(jnp.logical_and(which == b, level == layer_ref[b]), 1.0, onehot)
    for table in tables:
        table.wait()
    for ref, tab, rows in ((rot_out_t, u_tab, kout), (rot_in_t, v_tab, kin)):
        flat = dot_nt(onehot.astype(jnp.bfloat16), ref[...])
        for p in range(rows):
            piece = flat[:, p * rows:(p + 1) * rows]
            for b in range(blocks):
                tab[b, p:p + 1, :] = piece[b:b + 1, :]
    dot_nt_exact = functools.partial(
        lax.dot_general, dimension_numbers=(((1,), (1,)), ((), ())),
        precision=exact, preferred_element_type=jnp.float32,
    )
    eo = dot_nt_exact(onehot, eig_out_t[...])
    ei = dot_nt_exact(onehot, eig_in_t[...])
    inv_tab[...] = 1.0 / (dot_nn(eo, spread_out, exact) * dot_nn(ei, spread_in, exact) + DAMPING)

    def prepare(b):
        u_rows[...] = dot_nn(u_tab[b].astype(jnp.bfloat16), spread_out.astype(jnp.bfloat16))
        for p in range(kout):
            basis[p * kin:(p + 1) * kin, :] = (u_rows[p:p + 1, :] * spread_in).astype(jnp.bfloat16)
        v_wide = dot_nn(v_tab[b].astype(jnp.bfloat16), spread_group.astype(jnp.bfloat16))
        for o in range(reps):
            v_block[o * kin:(o + 1) * kin, :] = jnp.where(lane_group == o, v_wide, 0.0).astype(jnp.bfloat16)
        inverse = inv_tab[pl.ds(b, 1), :]
        for c in range(width // group):
            here = slice(c * group, (c + 1) * group)
            first = dot_nn(q_buf[b], basis[:, here]).astype(jnp.bfloat16)
            x2[:, here] = (dot_nn(first, v_block[...]) * inverse[:, here]).astype(jnp.bfloat16)
        for c in range(width // group):
            here = slice(c * group, (c + 1) * group)
            third = dot_nt(x2[...], basis[here, :]).astype(jnp.bfloat16)
            ready[b, :, here] = dot_nt(third, v_block[...]).astype(jnp.bfloat16)

    def forward(r, b):
        for d in range(2):
            @pl.when(receives(d, r, b))
            def _(d=d):
                hop(d, r, b).wait_recv()
            if r + 1 < n - 1:
                @pl.when(sends(d, r + 1, b))
                def _(d=d):
                    hop(d, r + 1, b).start()

    def multiply(r, b):
        for d in range(2):
            s = r + 1 if d == 0 else n - 1 - r
            @pl.when(receives(d, r, b))
            def _(d=d, s=s):
                acc[s] += dot_nt(slots[d, r, b], ready[b])

    def finish(r):
        for d in range(2):
            s = r + 1 if d == 0 else n - 1 - r
            @pl.when(receives(d, r, blocks - 1))
            def _(s=s):
                packed[s] = acc[s].astype(packed.dtype)
                send_part(s).start()

    def own(b, _):
        load_q(b).wait()
        load_g(b).wait()
        prepare(b)

        @pl.when(jnp.logical_and(is_end, b < moved))
        def _():
            far(b).start()

        forward(0, b)
        acc[0] += dot_nt(g_buf[b], ready[b])
        multiply(0, b)

        @pl.when(b >= blocks - 2)
        def _():
            for i in range(2):
                forward(1, (b - (blocks - 2)) * 2 + i)

        return 0

    def later(r):
        def body(b, _):
            if r == 1:
                @pl.when(b >= 4)
                def _():
                    forward(r, b)
            else:
                forward(r, b)
            multiply(r, b)
            return 0

        lax.fori_loop(0, blocks, body, 0)
        finish(r)

    lax.fori_loop(0, blocks, own, 0)

    @pl.when(f == 0)
    def _():
        parts[0] = acc[0].astype(parts.dtype)

    @pl.when(f != 0)
    def _():
        packed[0] = acc[0].astype(packed.dtype)
        send_part(0).start()

    finish(0)

    later(1)

    @pl.when(is_helper)
    def _():
        side = jnp.where(low, 0, 1)
        for m in range(moved):
            far(m).wait_recv()
            far_acc[0] += dot_nt(g_buf[m], far_ready[m])
            for r in range(n - 2):
                far_acc[1 + r] += dot_nt(slots[side, r, m], far_ready[m])

    for t in range(n - 1):
        here = jnp.logical_and(t == 0, far_feat(t) == f)

        @pl.when(jnp.logical_and(is_helper, here))
        def _(t=t):
            far_parts[pl.ds(f, 1)] = far_acc[t:t + 1].astype(far_parts.dtype)

        @pl.when(jnp.logical_and(is_helper, jnp.logical_not(here)))
        def _(t=t):
            far_packed[t] = far_acc[t].astype(far_packed.dtype)
            send_far_part(t).start()

    later(2)

    def arrived(ref, sem, h):
        return pltpu.make_async_remote_copy(
            src_ref=packed.at[0], dst_ref=ref.at[h],
            send_sem=part_send.at[0], recv_sem=sem.at[h],
            device_id=at(j, f), device_id_type=MESH,
        )

    k = lax.rem(j - f + n, n)
    split = jnp.logical_and(f != 0, jnp.logical_or(k == 0, k == n - 1))
    helper_of = jnp.where(k == 0, 1, n - 2)

    @pl.when(split)
    def _():
        for h in range(cols):
            @pl.when(jnp.logical_or(helper_of != j, h != f))
            def _(h=h):
                arrived(far_parts, far_part_recv, h).wait_recv()
        total = far_parts[0].astype(jnp.float32)
        for h in range(1, cols):
            total += far_parts[h].astype(jnp.float32)
        far_acc[n - 1] = total

    for h in range(cols):
        @pl.when(jnp.logical_not(jnp.logical_and(f == 0, h == 0)))
        def _(h=h):
            arrived(parts, part_recv, h).wait_recv()
    total = far_acc[n - 1] + parts[0].astype(jnp.float32)
    for h in range(1, cols):
        total += parts[h].astype(jnp.float32)
    acc[0] = total
    for r in range(examples):
        out_ref[r:r + 1, :] = acc[0, pl.ds(ids_ref[0, r], 1), :]

    @pl.when(f != 0)
    def _():
        send_part(0).wait_send()
    for s in range(1, n):
        send_part(s).wait_send()
    for t in range(n - 1):
        here = jnp.logical_and(t == 0, far_feat(t) == f)

        @pl.when(jnp.logical_and(is_helper, jnp.logical_not(here)))
        def _(t=t):
            send_far_part(t).wait_send()

    @pl.when(is_end)
    def _():
        for m in range(moved):
            far(m).wait_send()

    for r in range(n - 1):
        def drain(b, _):
            for d in range(2):
                @pl.when(sends(d, r, b))
                def _(d=d):
                    hop(d, r, b).wait_send()
            return 0

        lax.fori_loop(0, blocks, drain, 0)


def line_local(n, cols, queries, grads, example_ids, layer_of_block, rot_out, rot_in, eig_out, eig_in):
    rows = queries.shape[0]
    examples = grads.shape[0]
    blocks = layer_of_block.shape[0]
    layers, kout, kin = rot_out.shape[0], rot_out.shape[1], rot_in.shape[1]
    width = kout * kin
    group = min(256, width)
    moved = blocks // 4
    bf16, f32 = jnp.bfloat16, jnp.float32
    smem = pl.BlockSpec(memory_space=pltpu.SMEM)
    vmem = pl.BlockSpec(memory_space=pltpu.VMEM)
    hbm = pl.BlockSpec(memory_space=pl.ANY)
    dma = pltpu.SemaphoreType.DMA
    return pl.pallas_call(
        functools.partial(line_kernel, n, kout, kin, cols, moved),
        out_shape=jax.ShapeDtypeStruct((examples, rows), f32),
        in_specs=[smem, smem] + [hbm] * 6,
        out_specs=vmem,
        scratch_shapes=[
            pltpu.VMEM((kout * kout, layers), bf16),
            pltpu.VMEM((kin * kin, layers), bf16),
            pltpu.VMEM((kout, layers), f32),
            pltpu.VMEM((kin, layers), f32),
            pltpu.VMEM((blocks, kout, kout), f32),
            pltpu.VMEM((blocks, kin, kin), f32),
            pltpu.VMEM((blocks, width), f32),
            pltpu.VMEM((blocks, rows, width), bf16),
            pltpu.VMEM((blocks, rows, width), bf16),
            pltpu.VMEM((rows, width), bf16),
            pltpu.VMEM((width, width), bf16),
            pltpu.VMEM((kout, width), f32),
            pltpu.VMEM((group, group), bf16),
            pltpu.VMEM((blocks, examples, width), bf16),
            pltpu.VMEM((2, n - 1, blocks, examples, width), bf16),
            pltpu.VMEM((n, examples, rows), f32),
            pltpu.VMEM((cols, examples, rows), bf16),
            pltpu.VMEM((moved, rows, width), bf16),
            pltpu.VMEM((n, examples, rows), f32),
            pltpu.VMEM((cols, examples, rows), bf16),
            pltpu.VMEM((n, examples, rows), bf16),
            pltpu.VMEM((n - 1, examples, rows), bf16),
            dma((4,)),
            dma((blocks,)),
            dma((blocks,)),
            dma((2, n - 1, blocks)),
            dma((2, n - 1, blocks)),
            dma((n,)),
            dma((cols,)),
            dma((moved,)),
            dma((moved,)),
            dma((n - 1,)),
            dma((cols,)),
        ],
        compiler_params=pltpu.CompilerParams(
            collective_id=0, has_side_effects=True, vmem_limit_bytes=58 * 1024 * 1024
        ),
    )(
        layer_of_block, example_ids,
        rot_out.transpose(1, 2, 0).reshape(kout * kout, layers),
        rot_in.transpose(1, 2, 0).reshape(kin * kin, layers),
        eig_out.T, eig_in.T, queries, grads,
    )


def solution(mesh):
    in_specs = (
        P(("grp", "ex"), "feat"),
        P(("grp", "ex"), "feat"),
        P(("grp", "ex"), None),
        P("feat"),
        P(),
        P(),
        P(),
        P(),
    )
    out_specs = P(("grp", "ex"), "feat")
    n, cols = mesh.shape["ex"], mesh.shape["feat"]
    local = functools.partial(line_local, n, cols) if n == cols == STEPS + 1 else ring_local
    return jax.shard_map(local, mesh=mesh, in_specs=in_specs, out_specs=out_specs, check_vma=False)
```

```python
import functools

import jax
import jax.numpy as jnp
from jax import lax
from jax.experimental import pallas as pl
from jax.experimental.pallas import tpu as pltpu
from jax.sharding import PartitionSpec as P

STEPS = 3


DAMPING = 0.1

MESH = pl.DeviceIdType.MESH


def shifted(value, axis, steps):
    count = lax.axis_size(axis)
    pairs = [(source, (source + steps) % count) for source in range(count)]
    return lax.ppermute(value, axis, pairs)


def select_tables(layer_of_block, rot_out, rot_in, eig_out, eig_in):
    levels = jnp.arange(rot_out.shape[0], dtype=jnp.int32)
    onehot = layer_of_block[:, None] == levels[None, :]
    onehot_low = onehot.astype(jnp.bfloat16)
    onehot_full = onehot.astype(jnp.float32)
    out_basis = jnp.einsum(
        "bl,lpo->bpo", onehot_low, rot_out, preferred_element_type=jnp.float32
    ).astype(jnp.bfloat16)
    in_basis = jnp.einsum(
        "bl,lij->bij", onehot_low, rot_in, preferred_element_type=jnp.float32
    ).astype(jnp.bfloat16)
    out_vals = jnp.dot(onehot_full, eig_out, precision=lax.Precision.HIGHEST)
    in_vals = jnp.dot(onehot_full, eig_in, precision=lax.Precision.HIGHEST)
    inverse = 1.0 / (out_vals[:, :, None] * in_vals[:, None, :] + DAMPING)
    return (out_basis, in_basis, inverse)


def precondition(query_rows, out_basis, in_basis, inverse):
    rows = query_rows.shape[0]
    blocks = out_basis.shape[0]
    kout = out_basis.shape[1]
    kin = in_basis.shape[1]
    query_grid = query_rows.reshape(rows, blocks, kout, kin)
    first_rot = jnp.einsum(
        "bpo,nbpi->boin", out_basis, query_grid, preferred_element_type=jnp.float32
    ).astype(jnp.bfloat16)
    second_rot = (
        jnp.einsum("boin,bij->bojn", first_rot, in_basis, preferred_element_type=jnp.float32)
        * inverse[:, :, :, None]
    ).astype(jnp.bfloat16)
    third_rot = jnp.einsum(
        "bpo,bojn->bpjn", out_basis, second_rot, preferred_element_type=jnp.float32
    ).astype(jnp.bfloat16)
    ready = jnp.einsum(
        "bpjn,bij->nbpi", third_rot, in_basis, preferred_element_type=jnp.float32
    ).astype(jnp.bfloat16)
    return ready.reshape(rows, blocks * kout * kin)


def against(query_rows, grads):
    return lax.dot_general(
        query_rows, grads, (((1,), (1,)), ((), ())), preferred_element_type=jnp.float32
    )


def ring_local(queries, grads, example_ids, layer_of_block, rot_out, rot_in, eig_out, eig_in):
    out_basis, in_basis, inverse = select_tables(layer_of_block, rot_out, rot_in, eig_out, eig_in)
    ready = precondition(queries, out_basis, in_basis, inverse)
    current = grads
    pieces = []
    for offset in range(STEPS + 1):
        part = against(ready, current)
        pieces.append(shifted(part, "ex", offset) if offset else part)
        if offset < STEPS:
            current = shifted(current, "ex", -1)
    partial_value = jnp.concatenate(pieces, axis=0)
    owned_rows = lax.psum_scatter(partial_value, "feat", scatter_dimension=0, tiled=True)
    return jnp.take(owned_rows.T, example_ids[0], axis=0)


def dot_nt(a, b):
    return lax.dot_general(a, b, (((1,), (1,)), ((), ())), preferred_element_type=jnp.float32)


def dot_nn(a, b, precision=None):
    return jnp.dot(a, b, preferred_element_type=jnp.float32, precision=precision)


def line_kernel(
    n, kout, kin, cols, moved,
    layer_ref, ids_ref, rot_out_hbm, rot_in_hbm, eig_out_hbm, eig_in_hbm, q_hbm, g_hbm,
    out_ref,
    rot_out_t, rot_in_t, eig_out_t, eig_in_t, u_tab, v_tab, inv_tab,
    q_buf, ready, x2, basis, u_rows, v_block, g_buf, slots, acc, parts,
    far_ready, far_acc, far_parts, packed, far_packed,
    table_sem, q_sem, g_sem, send_sem, recv_sem, part_send, part_recv,
    far_send, far_recv, far_part_send, far_part_recv,
):
    j = lax.axis_index("ex")
    f = lax.axis_index("feat")
    blocks = ready.shape[0]
    width = kout * kin
    examples = g_buf.shape[1]
    layers = rot_out_t.shape[1]
    exact = lax.Precision.HIGHEST

    def at(ex, feat):
        return {"ex": ex, "feat": feat}

    def hbm_block(ref, b):
        if not isinstance(b, int):
            b = pl.multiple_of(b * width, width)
        else:
            b = b * width
        return ref.at[:, pl.ds(b, width)]

    def load_q(b):
        return pltpu.make_async_copy(hbm_block(q_hbm, b), q_buf.at[b], q_sem.at[b])

    def load_g(b):
        return pltpu.make_async_copy(hbm_block(g_hbm, b), g_buf.at[b], g_sem.at[b])

    def hop(d, r, b):
        src = hbm_block(g_hbm, b) if r == 0 else slots.at[d, r - 1, b]
        to = jnp.maximum(j - 1, 0) if d == 0 else jnp.minimum(j + 1, n - 1)
        return pltpu.make_async_remote_copy(
            src_ref=src, dst_ref=slots.at[d, r, b],
            send_sem=send_sem.at[d, r, b], recv_sem=recv_sem.at[d, r, b],
            device_id=at(to, f), device_id_type=MESH,
        )

    def sends(d, r, b):
        if d == 0:
            there = jnp.logical_and(j > 0, j + r <= n - 1)
            return jnp.logical_and(there, jnp.logical_or(j != 1, b >= moved))
        there = jnp.logical_and(j < n - 1, j - r >= 0)
        return jnp.logical_and(there, jnp.logical_or(j != n - 2, b >= moved))

    def receives(d, r, b):
        if d == 0:
            return jnp.logical_and(j + 1 + r <= n - 1, jnp.logical_or(j != 0, b >= moved))
        return jnp.logical_and(j - 1 - r >= 0, jnp.logical_or(j != n - 1, b >= moved))

    def far(m):
        return pltpu.make_async_remote_copy(
            src_ref=ready.at[m], dst_ref=far_ready.at[m],
            send_sem=far_send.at[m], recv_sem=far_recv.at[m],
            device_id=at(jnp.where(j < 2, 1, n - 2), f), device_id_type=MESH,
        )

    is_end = jnp.logical_or(j == 0, j == n - 1)
    is_helper = jnp.logical_or(j == 1, j == n - 2)
    low = j == 1

    def send_part(s):
        return pltpu.make_async_remote_copy(
            src_ref=packed.at[s], dst_ref=parts.at[f],
            send_sem=part_send.at[s], recv_sem=part_recv.at[f],
            device_id=at(lax.rem(j + s, n), s), device_id_type=MESH,
        )

    def far_feat(t):
        return jnp.where(low, 1 + t, n - 1 - t)

    def send_far_part(t):
        return pltpu.make_async_remote_copy(
            src_ref=far_packed.at[t], dst_ref=far_parts.at[f],
            send_sem=far_part_send.at[t], recv_sem=far_part_recv.at[f],
            device_id=at(jnp.where(low, 1 + t, n - 2 - t), far_feat(t)), device_id_type=MESH,
        )

    tables = [
        pltpu.make_async_copy(src, dst, table_sem.at[i])
        for i, (src, dst) in enumerate([
            (rot_out_hbm, rot_out_t), (rot_in_hbm, rot_in_t),
            (eig_out_hbm, eig_out_t), (eig_in_hbm, eig_in_t),
        ])
    ]

    barrier = pltpu.get_barrier_semaphore()
    for e in range(n):
        for h in range(cols):
            @pl.when(jnp.logical_or(e != j, h != f))
            def _():
                pl.semaphore_signal(barrier, inc=1, device_id=at(e, h), device_id_type=MESH)
    for table in tables:
        table.start()
    for b in range(blocks):
        load_q(b).start()
        load_g(b).start()
    pl.semaphore_wait(barrier, n * cols - 1)

    for b in range(blocks):
        for d in range(2):
            @pl.when(sends(d, 0, b))
            def _(d=d, b=b):
                hop(d, 0, b).start()

    acc[...] = jnp.zeros_like(acc)
    far_acc[...] = jnp.zeros_like(far_acc)

    lane = lax.broadcasted_iota(jnp.int32, (kout, width), 1)
    row = lax.broadcasted_iota(jnp.int32, (kout, width), 0)
    spread_out = (lane // kin == row).astype(jnp.float32)
    spread_in = (lane % kin == row).astype(jnp.float32)
    group = v_block.shape[0]
    reps = group // kin
    lane_group = lax.broadcasted_iota(jnp.int32, (kin, group), 1) // kin
    spread_group = spread_in[:, :group]

    level = lax.broadcasted_iota(jnp.int32, (blocks, layers), 1)
    which = lax.broadcasted_iota(jnp.int32, (blocks, layers), 0)
    onehot = jnp.zeros((blocks, layers), jnp.float32)
    for b in range(blocks):
        onehot = jnp.where(jnp.logical_and(which == b, level == layer_ref[b]), 1.0, onehot)
    for table in tables:
        table.wait()
    for ref, tab, rows in ((rot_out_t, u_tab, kout), (rot_in_t, v_tab, kin)):
        flat = dot_nt(onehot.astype(jnp.bfloat16), ref[...])
        for p in range(rows):
            piece = flat[:, p * rows:(p + 1) * rows]
            for b in range(blocks):
                tab[b, p:p + 1, :] = piece[b:b + 1, :]
    dot_nt_exact = functools.partial(
        lax.dot_general, dimension_numbers=(((1,), (1,)), ((), ())),
        precision=exact, preferred_element_type=jnp.float32,
    )
    eo = dot_nt_exact(onehot, eig_out_t[...])
    ei = dot_nt_exact(onehot, eig_in_t[...])
    inv_tab[...] = 1.0 / (dot_nn(eo, spread_out, exact) * dot_nn(ei, spread_in, exact) + DAMPING)

    def prepare(b):
        u_rows[...] = dot_nn(u_tab[b].astype(jnp.bfloat16), spread_out.astype(jnp.bfloat16))
        for p in range(kout):
            basis[p * kin:(p + 1) * kin, :] = (u_rows[p:p + 1, :] * spread_in).astype(jnp.bfloat16)
        v_wide = dot_nn(v_tab[b].astype(jnp.bfloat16), spread_group.astype(jnp.bfloat16))
        for o in range(reps):
            v_block[o * kin:(o + 1) * kin, :] = jnp.where(lane_group == o, v_wide, 0.0).astype(jnp.bfloat16)
        inverse = inv_tab[pl.ds(b, 1), :]
        for c in range(width // group):
            here = slice(c * group, (c + 1) * group)
            first = dot_nn(q_buf[b], basis[:, here]).astype(jnp.bfloat16)
            x2[:, here] = (dot_nn(first, v_block[...]) * inverse[:, here]).astype(jnp.bfloat16)
        for c in range(width // group):
            here = slice(c * group, (c + 1) * group)
            third = dot_nt(x2[...], basis[here, :]).astype(jnp.bfloat16)
            ready[b, :, here] = dot_nt(third, v_block[...]).astype(jnp.bfloat16)

    def forward(r, b):
        for d in range(2):
            @pl.when(receives(d, r, b))
            def _(d=d):
                hop(d, r, b).wait_recv()
            if r + 1 < n - 1:
                @pl.when(sends(d, r + 1, b))
                def _(d=d):
                    hop(d, r + 1, b).start()

    def multiply(r, b):
        for d in range(2):
            s = r + 1 if d == 0 else n - 1 - r
            @pl.when(receives(d, r, b))
            def _(d=d, s=s):
                acc[s] += dot_nt(slots[d, r, b], ready[b])

    def finish(r):
        for d in range(2):
            s = r + 1 if d == 0 else n - 1 - r
            @pl.when(receives(d, r, blocks - 1))
            def _(s=s):
                packed[s] = acc[s].astype(packed.dtype)
                send_part(s).start()

    def own(b, _):
        load_q(b).wait()
        load_g(b).wait()
        prepare(b)

        @pl.when(jnp.logical_and(is_end, b < moved))
        def _():
            far(b).start()

        for i in range(blocks):
            @pl.when(b == i)
            def _(i=i):
                for c in range(i * 3 // 2, (i + 1) * 3 // 2):
                    forward(c // blocks, c % blocks)

        acc[0] += dot_nt(g_buf[b], ready[b])
        multiply(0, b)
        return 0

    def later(r):
        def body(b, _):
            if r == 1:
                @pl.when(b >= blocks * 3 // 2 - blocks)
                def _():
                    forward(r, b)
            else:
                forward(r, b)
            multiply(r, b)
            return 0

        lax.fori_loop(0, blocks, body, 0)
        finish(r)

    lax.fori_loop(0, blocks, own, 0)

    @pl.when(f == 0)
    def _():
        parts[0] = acc[0].astype(parts.dtype)

    @pl.when(f != 0)
    def _():
        packed[0] = acc[0].astype(packed.dtype)
        send_part(0).start()

    finish(0)

    later(1)

    @pl.when(is_helper)
    def _():
        side = jnp.where(low, 0, 1)
        for m in range(moved):
            far(m).wait_recv()
            far_acc[0] += dot_nt(g_buf[m], far_ready[m])
            for r in range(n - 2):
                far_acc[1 + r] += dot_nt(slots[side, r, m], far_ready[m])

    for t in range(n - 1):
        here = jnp.logical_and(t == 0, far_feat(t) == f)

        @pl.when(jnp.logical_and(is_helper, here))
        def _(t=t):
            far_parts[pl.ds(f, 1)] = far_acc[t:t + 1].astype(far_parts.dtype)

        @pl.when(jnp.logical_and(is_helper, jnp.logical_not(here)))
        def _(t=t):
            far_packed[t] = far_acc[t].astype(far_packed.dtype)
            send_far_part(t).start()

    later(2)

    def arrived(ref, sem, h):
        return pltpu.make_async_remote_copy(
            src_ref=packed.at[0], dst_ref=ref.at[h],
            send_sem=part_send.at[0], recv_sem=sem.at[h],
            device_id=at(j, f), device_id_type=MESH,
        )

    k = lax.rem(j - f + n, n)
    split = jnp.logical_and(f != 0, jnp.logical_or(k == 0, k == n - 1))
    helper_of = jnp.where(k == 0, 1, n - 2)

    @pl.when(split)
    def _():
        for h in range(cols):
            @pl.when(jnp.logical_or(helper_of != j, h != f))
            def _(h=h):
                arrived(far_parts, far_part_recv, h).wait_recv()
        total = far_parts[0].astype(jnp.float32)
        for h in range(1, cols):
            total += far_parts[h].astype(jnp.float32)
        far_acc[n - 1] = total

    for h in range(cols):
        @pl.when(jnp.logical_not(jnp.logical_and(f == 0, h == 0)))
        def _(h=h):
            arrived(parts, part_recv, h).wait_recv()
    total = far_acc[n - 1] + parts[0].astype(jnp.float32)
    for h in range(1, cols):
        total += parts[h].astype(jnp.float32)
    acc[0] = total
    for r in range(examples):
        out_ref[r:r + 1, :] = acc[0, pl.ds(ids_ref[0, r], 1), :]

    @pl.when(f != 0)
    def _():
        send_part(0).wait_send()
    for s in range(1, n):
        send_part(s).wait_send()
    for t in range(n - 1):
        here = jnp.logical_and(t == 0, far_feat(t) == f)

        @pl.when(jnp.logical_and(is_helper, jnp.logical_not(here)))
        def _(t=t):
            send_far_part(t).wait_send()

    @pl.when(is_end)
    def _():
        for m in range(moved):
            far(m).wait_send()

    for r in range(n - 1):
        def drain(b, _):
            for d in range(2):
                @pl.when(sends(d, r, b))
                def _(d=d):
                    hop(d, r, b).wait_send()
            return 0

        lax.fori_loop(0, blocks, drain, 0)


def line_local(n, cols, queries, grads, example_ids, layer_of_block, rot_out, rot_in, eig_out, eig_in):
    rows = queries.shape[0]
    examples = grads.shape[0]
    blocks = layer_of_block.shape[0]
    layers, kout, kin = rot_out.shape[0], rot_out.shape[1], rot_in.shape[1]
    width = kout * kin
    group = min(256, width)
    moved = blocks // 4
    bf16, f32 = jnp.bfloat16, jnp.float32
    smem = pl.BlockSpec(memory_space=pltpu.SMEM)
    vmem = pl.BlockSpec(memory_space=pltpu.VMEM)
    hbm = pl.BlockSpec(memory_space=pl.ANY)
    dma = pltpu.SemaphoreType.DMA
    return pl.pallas_call(
        functools.partial(line_kernel, n, kout, kin, cols, moved),
        out_shape=jax.ShapeDtypeStruct((examples, rows), f32),
        in_specs=[smem, smem] + [hbm] * 6,
        out_specs=vmem,
        scratch_shapes=[
            pltpu.VMEM((kout * kout, layers), bf16),
            pltpu.VMEM((kin * kin, layers), bf16),
            pltpu.VMEM((kout, layers), f32),
            pltpu.VMEM((kin, layers), f32),
            pltpu.VMEM((blocks, kout, kout), f32),
            pltpu.VMEM((blocks, kin, kin), f32),
            pltpu.VMEM((blocks, width), f32),
            pltpu.VMEM((blocks, rows, width), bf16),
            pltpu.VMEM((blocks, rows, width), bf16),
            pltpu.VMEM((rows, width), bf16),
            pltpu.VMEM((width, width), bf16),
            pltpu.VMEM((kout, width), f32),
            pltpu.VMEM((group, group), bf16),
            pltpu.VMEM((blocks, examples, width), bf16),
            pltpu.VMEM((2, n - 1, blocks, examples, width), bf16),
            pltpu.VMEM((n, examples, rows), f32),
            pltpu.VMEM((cols, examples, rows), bf16),
            pltpu.VMEM((moved, rows, width), bf16),
            pltpu.VMEM((n, examples, rows), f32),
            pltpu.VMEM((cols, examples, rows), bf16),
            pltpu.VMEM((n, examples, rows), bf16),
            pltpu.VMEM((n - 1, examples, rows), bf16),
            dma((4,)),
            dma((blocks,)),
            dma((blocks,)),
            dma((2, n - 1, blocks)),
            dma((2, n - 1, blocks)),
            dma((n,)),
            dma((cols,)),
            dma((moved,)),
            dma((moved,)),
            dma((n - 1,)),
            dma((cols,)),
        ],
        compiler_params=pltpu.CompilerParams(
            collective_id=0, has_side_effects=True, vmem_limit_bytes=58 * 1024 * 1024
        ),
    )(
        layer_of_block, example_ids,
        rot_out.transpose(1, 2, 0).reshape(kout * kout, layers),
        rot_in.transpose(1, 2, 0).reshape(kin * kin, layers),
        eig_out.T, eig_in.T, queries, grads,
    )


def solution(mesh):
    in_specs = (
        P(("grp", "ex"), "feat"),
        P(("grp", "ex"), "feat"),
        P(("grp", "ex"), None),
        P("feat"),
        P(),
        P(),
        P(),
        P(),
    )
    out_specs = P(("grp", "ex"), "feat")
    n, cols = mesh.shape["ex"], mesh.shape["feat"]
    local = functools.partial(line_local, n, cols) if n == cols == STEPS + 1 else ring_local
    return jax.shard_map(local, mesh=mesh, in_specs=in_specs, out_specs=out_specs, check_vma=False)
```
